32 devices in a mesh: groups: 2 (over y), mesh: 8 (over z, x), layer: 2 (over core).
Axes of the slice: x: 2, y: 2, z: 4, core: 2. Of those that a mesh axis runs over, the one named last changes fastest.
Arguments:
- displacement: float32 [3, 16384], P(None, ('groups', 'mesh', 'layer')), parts along dimension 1, may hold values from -6 to 6
- tangent_one: float32 [3, 16384], P(None, ('groups', 'mesh', 'layer')), parts along dimension 1, may hold values from -6 to 6
- tangent_two: float32 [3, 16384], P(None, ('groups', 'mesh', 'layer')), parts along dimension 1, may hold values from -6 to 6
- external_force: float32 [3, 16384], P(None, ('groups', 'mesh', 'layer')), parts along dimension 1, may hold values from -6 to 6
- connectivity: int32 [8, 4096], P(None, ('groups', 'mesh', 'layer')), parts along dimension 1, may hold values from 0 to 543
- element_scale: float32 [4096], P(('groups', 'mesh', 'layer')), parts along dimension 0, may hold values from 0.3 to 3
- halo_nodes: int32 [1024], P(('groups', 'mesh', 'layer')), parts along dimension 0, may hold values from 0 to 511
- slave_nodes: int32 [2048, 128], P(('groups', 'mesh', 'layer')), parts along dimension 0, may hold values from 0 to 512, as said below
- master_nodes: int32 [2048, 128], P(('groups', 'mesh', 'layer')), parts along dimension 0, may hold values from 0 to 512, as said below
- pair_owner: int32 [2048, 1], P(('groups', 'mesh', 'layer')), parts along dimension 0, may hold values from 0 to 15; in each aligned block of 64 rows (0 to 63, 64 to 127, ...) at most 8 rows name the same one
- pair_slot: int32 [2048], P(('groups', 'mesh', 'layer')), parts along dimension 0, may hold values from 0 to 63
- active_flags: int32 [2048, 128], P(('groups', 'mesh', 'layer')), parts along dimension 0, may hold values 0 or 1
- normals: float32 [2048, 3], P(('groups', 'mesh', 'layer')), parts along dimension 0, may hold values from -1 to 1
- initial_gap: float32 [2048, 128], P(('groups', 'mesh', 'layer')), parts along dimension 0, may hold values from -6 to 6
- strain_operator: float32 [48, 24], replicated, may hold values from -1.25 to 1.25
- mortar: float32 [128, 128], replicated
Outputs:
- residual: float32 [3, 16384], P(None, ('groups', 'mesh', 'layer')), parts along dimension 1
- jvp_one: float32 [3, 16384], P(None, ('groups', 'mesh', 'layer')), parts along dimension 1
- jvp_two: float32 [3, 16384], P(None, ('groups', 'mesh', 'layer')), parts along dimension 1
The draws below stay inside these ranges and needn't reach their ends.
There are 2 independent parts, one for each index of `groups`. The reference program is written for one: setup_inputs(seed, part) draws one part's arguments, and reference() takes and returns one part's arrays. A program takes and returns all parts, laid end to end along the dimension named above; an argument that names none is the same for every part. Nothing has to cross between parts.
Inputs may be any that keep to these rules, and one draw needn't show every extreme that they name: `slave_nodes`: each row holds one slave patch's node numbers on its own device, real nodes first, then padding with the value 512; every patch has half of 128 real nodes or more. `master_nodes`: each row holds one master patch's node numbers on its owner device, real nodes first, then padding with the value 512; every patch has half of 128 real nodes or more. `pair_owner`: among the slave patches of one device at most 8 name the same owner, a bound that some block reaches. `halo_nodes`: node numbers of the device that holds the list. `connectivity`: numbers below 512 are the device's own nodes; the others are its ghosts in order.
All inputs are finite; a program needn't handle non-finite values. No bound on the sum of `active_flags` on one device may be relied on, other than what follows from the above.
Results may differ from the reference program's by a relative error of at most 0.00005.
Values sent between devices are 32-bit elements; how exact they have to be, the bound alone decides.
A program may use at most 64 MiB of HBM per device.

```python
import math
import jax
import jax.numpy as jnp
import numpy as np
from jax import lax

NODE_DEV = 512
ELEM_DEV = 128
SLAVE_DEV = 64
PATCH = 128
STRAINS = 48
ELEM_DOF = 24
DEV_PART = 16
GHOST = 32
MASTER_DEV = 64
CAP = 8
NODES = 8192
ELEMS = 2048
SLAVES = 1024
MASTERS = 1024


def patch_indices(key, row_count):
    key_count, key_index = jax.random.split(key)
    counts = jax.random.randint(key_count, (row_count, 1), PATCH // 2, PATCH + 1)
    counts = counts.at[0, 0].set(PATCH).at[1, 0].set(PATCH // 2)
    indices = jax.random.randint(key_index, (row_count, PATCH), 0, NODE_DEV)
    return jnp.where(jnp.arange(PATCH)[None, :] < counts, indices, NODE_DEV).astype(jnp.int32)


def draw_slave_nodes(key, part):
    key = jax.random.fold_in(key, 11)
    return patch_indices(key, SLAVES)


def draw_master_nodes(key, part):
    key = jax.random.fold_in(key, 12)
    return patch_indices(key, MASTERS)


def draw_mortar(key, part):
    key = jax.random.fold_in(key, 13)
    noise = jax.random.normal(key, (PATCH, PATCH), jnp.float32)
    return (jnp.eye(PATCH, dtype=jnp.float32) + 0.3 * noise / jnp.sqrt(jnp.float32(PATCH))).astype(jnp.float32)


def plant(drawn, key, low, high):
    spot = [jax.random.randint(jax.random.fold_in(key, axis), (), 0, length) for axis, length in enumerate(drawn.shape)]
    longest = drawn.shape.index(max(drawn.shape))
    beside = spot[:longest] + [(spot[longest] + 1) % drawn.shape[longest]] + spot[longest + 1:]
    return drawn.at[tuple(spot)].set(low).at[tuple(beside)].set(high)


def block_scale(key, dims, shards, low, top_value):
    def one(position, blocks):
        steps = jax.random.uniform(jax.random.fold_in(jax.random.fold_in(key, 6), position), (blocks,), jnp.float32, low / len(shards), top_value / len(shards))
        return jnp.repeat(jnp.exp(steps), dims[position] // blocks).reshape((-1,) + (1,) * (len(dims) - position - 1))

    factor_of = one(*shards[0])
    for cut in shards[1:]:
        factor_of = factor_of * one(*cut)
    return factor_of


def shared_out(stream_key, own, number, rows, count, top, limit, skew):
    order = jax.random.permutation(stream_key, count)
    packed, ordinary = portions_of(count, rows * top, limit, skew, True), portions_of(count, rows * top, limit, skew, False)
    places = jnp.arange(count)

    def named(sizes, offset_by):
        used = int((sizes > 0).sum())
        fixed = max(1, used // 4)
        passed = fixed + (places - fixed + offset_by * (used - fixed)) % max(1, count - fixed)
        return jnp.zeros((count,), jnp.int32).at[order[jnp.where(places < fixed, places, passed)]].set(jnp.asarray(sizes, jnp.int32))

    sizes = jnp.where(number % 4 == 0, named(packed, number // 4), named(ordinary, number - number // 4 - 1))
    mixed = jax.random.permutation(jax.random.fold_in(own, 3), count)
    donor, receiver = mixed[0:count // 2 * 2:2], mixed[1:count // 2 * 2:2]
    slack = jnp.minimum(sizes[donor] - 1, limit - sizes[receiver]) // 2
    slack = jnp.where((donor == order[0]) | (receiver == order[0]) | (sizes[receiver] == 0), 0, jnp.maximum(slack, 0))
    passed = jax.random.randint(jax.random.fold_in(own, 4), (count // 2,), 0, 1 << 20) % (slack + 1)
    sizes = sizes.at[donor].add(-passed).at[receiver].add(passed)
    items = jnp.searchsorted(jnp.cumsum(sizes), jnp.arange(rows * top), side="right").astype(jnp.int32)
    table = items.reshape(top, rows).T
    table = table[jax.random.permutation(jax.random.fold_in(own, 1), rows)]
    offset_by = jax.random.randint(jax.random.fold_in(own, 2), (rows, 1), 0, top)
    return jnp.take_along_axis(table, (jnp.arange(top)[None, :] + offset_by) % top, axis=1)


def portions_of(count, total, limit, lean, full):
    portions = [(1 << 20) // math.isqrt(grade ** lean) + 1 for grade in range(1, count + 1)]
    largest = limit if full else min(limit, max(-(-total // count), total * portions[0] // sum(portions)))
    least = 1 if total - largest >= count - 1 else 0
    given, spare = [largest] + [least] * (count - 1), total - largest - least * (count - 1)
    while spare > 0:
        movable = [i for i in range(1, count) if given[i] < largest] or [i for i in range(1, count) if given[i] < limit]
        mass, left = sum([portions[i] for i in movable]), spare
        for i in movable:
            addition = min(limit - given[i], max(1, left * portions[i] // mass), spare)
            given[i] = given[i] + addition
            spare = spare - addition
    return np.array(given)


def gaussian(stream_key, dims, scale, reach, cuts=(), kind=jnp.bfloat16):
    values = scale * jax.random.normal(stream_key, dims, jnp.float32)
    if cuts:
        values = values * block_scale(stream_key, dims, cuts, -0.22, 0.18)
    return jnp.clip(values, -reach, reach).astype(kind)


def setup_inputs(seed: int = 0, part: int = 0) -> dict:
    splits = jax.random.split(jax.random.key(seed), 17)
    own_keys = jax.random.split(jax.random.fold_in(splits[16], part), 17)
    displacement = gaussian(own_keys[0], (3, NODES), 1.0, 6.0, ((1, 16),), jnp.float32)
    tangent_one = gaussian(own_keys[1], (3, NODES), 1.0, 6.0, ((1, 16),), jnp.float32)
    tangent_two = gaussian(own_keys[2], (3, NODES), 1.0, 6.0, ((1, 16),), jnp.float32)
    external_force = gaussian(own_keys[3], (3, NODES), 1.0, 6.0, ((1, 16),), jnp.float32)
    connectivity = plant(jax.random.randint(own_keys[4], (8, ELEMS), 0, NODE_DEV + GHOST), jax.random.fold_in(own_keys[4], 1), 0, (NODE_DEV + GHOST) - 1).astype(jnp.int32)
    element_scale = jnp.clip(jnp.exp(math.log(3.0) - 2.3025851 * jax.random.uniform(own_keys[5], (ELEMS,), jnp.float32) ** block_scale(own_keys[5], (ELEMS,), ((0, 16),), -0.2, 0.2)), 0.3, 3.0)
    halo_nodes = plant(jax.random.randint(own_keys[6], (GHOST * DEV_PART,), 0, NODE_DEV), jax.random.fold_in(own_keys[6], 1), 0, NODE_DEV - 1).astype(jnp.int32)
    slave_nodes = draw_slave_nodes(jax.random.fold_in(jax.random.fold_in(splits[16], part), 71), part)
    master_nodes = draw_master_nodes(jax.random.fold_in(jax.random.fold_in(splits[16], part), 71), part)
    pair_owner_keys = jax.random.split(jax.random.fold_in(own_keys[9], 1), SLAVES // SLAVE_DEV)
    pair_owner_turns = jax.random.permutation(jax.random.fold_in(own_keys[9], 3), SLAVES // SLAVE_DEV)
    pair_owner = jax.vmap(lambda own, number: shared_out(jax.random.fold_in(own_keys[9], 2), own, number, SLAVE_DEV, DEV_PART, 1, CAP, 2))(pair_owner_keys, pair_owner_turns).reshape((SLAVES, 1))
    pair_slot = plant(jax.random.randint(own_keys[10], (SLAVES,), 0, MASTER_DEV), jax.random.fold_in(own_keys[10], 1), 0, MASTER_DEV - 1).astype(jnp.int32)
    active_flags = plant((jax.random.randint(own_keys[11], (SLAVES, PATCH), 0, 4) < 3).astype(jnp.int32), jax.random.fold_in(own_keys[11], 1), 0, 1)
    normals = jnp.clip(jax.random.uniform(own_keys[12], (SLAVES, 3), jnp.float32, -1.0, 1.0) * block_scale(own_keys[12], (SLAVES, 3), ((0, 16),), -0.4, 0.0), -1.0, 1.0)
    initial_gap = gaussian(own_keys[13], (SLAVES, PATCH), 1.0, 6.0, ((0, 16),), jnp.float32)
    strain_operator = gaussian(splits[14], (STRAINS, ELEM_DOF), ELEM_DOF ** -0.5, 1.25, (), jnp.float32)
    mortar = draw_mortar(jax.random.fold_in(splits[16], 71), part)
    return {"displacement": displacement, "tangent_one": tangent_one, "tangent_two": tangent_two, "external_force": external_force, "connectivity": connectivity, "element_scale": element_scale, "halo_nodes": halo_nodes, "slave_nodes": slave_nodes, "master_nodes": master_nodes, "pair_owner": pair_owner, "pair_slot": pair_slot, "active_flags": active_flags, "normals": normals, "initial_gap": initial_gap, "strain_operator": strain_operator, "mortar": mortar}


PENALTY = 2.0
HIGH = lax.Precision.HIGHEST


def element_forces(extended, corners, scale, operator):
    element_values = jnp.transpose(extended[:, corners], (1, 0, 2)).reshape(24, -1)
    strain = jnp.dot(operator, element_values, precision=HIGH)
    stress = scale * (strain + 0.5 * jnp.tanh(strain))
    element_force = jnp.dot(operator.T, stress, precision=HIGH).reshape(8, 3, -1)
    element_force = jnp.transpose(element_force, (1, 0, 2))
    return jnp.zeros((3, extended.shape[1]), extended.dtype).at[:, corners].add(element_force)


def reference(displacement, tangent_one, tangent_two, external_force, connectivity, element_scale, halo_nodes, slave_nodes, master_nodes, pair_owner, pair_slot, active_flags, normals, initial_gap, strain_operator, mortar):
    halo_table = halo_nodes.reshape(DEV_PART, GHOST)
    corner_table = jnp.transpose(connectivity.reshape(8, DEV_PART, ELEM_DEV), (1, 0, 2))
    scale_table = element_scale.reshape(DEV_PART, ELEM_DEV)
    slave_device = (jnp.arange(SLAVES, dtype=jnp.int32) // SLAVE_DEV).astype(jnp.int32)
    slave_index = slave_device[:, None] * (NODE_DEV + 1) + slave_nodes
    owners = pair_owner[:, 0]
    master_id = owners * MASTER_DEV + pair_slot
    master_index = owners[:, None] * (NODE_DEV + 1) + master_nodes[master_id]
    live_mask = (slave_nodes < NODE_DEV).astype(normals.dtype)
    contact_weight = PENALTY * active_flags.astype(normals.dtype) * live_mask
    normal_rows = normals.T

    def residual_of(field):
        by_device = jnp.transpose(field.reshape(3, DEV_PART, NODE_DEV), (1, 0, 2))
        outgoing = jax.vmap(lambda values, table: values[:, table])(by_device, halo_table)
        ghosts = jnp.roll(outgoing, -1, axis=0)
        extended = jnp.concatenate([by_device, ghosts], axis=2)
        internal = lax.map(lambda items: element_forces(items[0], items[1], items[2], strain_operator), (extended, corner_table, scale_table))
        owned = internal[:, :, :NODE_DEV]
        returned = jnp.roll(internal[:, :, NODE_DEV:], 1, axis=0)
        owned = jax.vmap(lambda values, table, extra: values.at[:, table].add(extra))(owned, halo_table, returned)
        padded = jnp.concatenate([by_device, jnp.zeros((DEV_PART, 3, 1), field.dtype)], axis=2)
        flattened = jnp.transpose(padded, (1, 0, 2)).reshape(3, DEV_PART * (NODE_DEV + 1))
        slave_values = flattened[:, slave_index]
        master_values = flattened[:, master_index]
        projected = jnp.dot(master_values.reshape(-1, PATCH), mortar.T, precision=HIGH).reshape(3, SLAVES, PATCH)
        gap_now = initial_gap + jnp.sum(normal_rows[:, :, None] * (slave_values - projected), axis=0)
        multiplier = contact_weight * jax.nn.softplus(-gap_now)
        slave_force = -normal_rows[:, :, None] * multiplier[None, :, :]
        spread = jnp.dot(multiplier, mortar, precision=HIGH)
        master_force = normal_rows[:, :, None] * spread[None, :, :]
        contact = jnp.zeros((3, DEV_PART * (NODE_DEV + 1)), field.dtype)
        contact = contact.at[:, slave_index].add(slave_force).at[:, master_index].add(master_force)
        contact = contact.reshape(3, DEV_PART, NODE_DEV + 1)[:, :, :NODE_DEV].reshape(3, NODES)
        internal_all = jnp.transpose(owned, (1, 0, 2)).reshape(3, NODES)
        return internal_all + contact - external_force

    residual, jvp_one = jax.jvp(residual_of, (displacement,), (tangent_one,))
    unused, jvp_two = jax.jvp(residual_of, (displacement,), (tangent_two,))
    return residual, jvp_one, jvp_two
```

```python
import functools

import jax
import jax.numpy as jnp
from jax import lax
from jax.experimental import pallas as pl
from jax.experimental.pallas import tpu as pltpu
from jax.sharding import PartitionSpec as P

PENALTY = 2.0
HIGH = lax.Precision.HIGHEST
LANES = 128
ROWS = 16
FIELDS = 3
NN = ((1,), (0,))
NT = ((1,), (1,))
TN = ((0,), (0,))
F32 = jnp.float32
BF16 = jnp.bfloat16


def dot(left, right, dims):
    return lax.dot_general(
        left, right, (dims, ((), ())), precision=HIGH, preferred_element_type=F32
    )


def dot16(left, right, dims):
    return lax.dot_general(left, right, (dims, ((), ())), preferred_element_type=F32)


def halves(value):
    top = value.astype(BF16)
    return top, (value - top.astype(F32)).astype(BF16)


def thirds(value):
    top = value.astype(BF16)
    rest = value - top.astype(F32)
    middle = rest.astype(BF16)
    return top, middle, (rest - middle.astype(F32)).astype(BF16)


def iota(shape, dim):
    return lax.broadcasted_iota(jnp.int32, shape, dim)


def where01(mask):
    return jnp.where(mask, 1.0, 0.0).astype(F32)


def column(index, by=LANES):
    return slice(index * by, (index + 1) * by)


def lookup(tile_of, tiles, index):
    lane = jnp.bitwise_and(index, LANES - 1)
    tile = jnp.right_shift(index, 7)
    found = jnp.zeros(index.shape, F32)
    for number in range(tiles):
        table = jnp.broadcast_to(tile_of(number), index.shape)
        picked = jnp.take_along_axis(table, lane, axis=1, mode="promise_in_bounds")
        found = jnp.where(tile == number, picked, found)
    return found


def add_operands(values, index, tiles):
    lane = jnp.bitwise_and(index, LANES - 1)
    tile = jnp.right_shift(index, 7)
    top = values.astype(BF16).astype(F32)
    both = jnp.concatenate([top, values - top], axis=0)
    left = jnp.concatenate(
        [jnp.where(tile == number, both, 0.0).astype(BF16) for number in range(tiles)], axis=0
    )
    right = where01(lane == iota((LANES, LANES), 0)).astype(BF16)
    return left, right


def add_rows(value_ref, index_ref, first, groups, tiles, total):
    def step(group, total):
        rows = index_ref[pl.ds(pl.multiple_of(group * 8, 8), 8), :]
        pairs = [
            add_operands(value_ref[first + group * 8 + k], rows[k : k + 1, :], tiles)
            for k in range(8)
        ]
        left = jnp.concatenate([pair[0] for pair in pairs], axis=1)
        right = jnp.concatenate([pair[1] for pair in pairs], axis=1)
        return total + dot16(left, right, NT)

    return lax.fori_loop(0, groups, step, total)


def tile_sum(total, number):
    start = number * 2 * ROWS
    return total[start : start + ROWS] + total[start + ROWS : start + 2 * ROWS]


def kernel(
    devices,
    layers,
    share,
    displacement,
    tangent_one,
    tangent_two,
    external_force,
    connectivity,
    element_scale,
    halo_nodes,
    slave_nodes,
    master_nodes,
    pair_owner,
    pair_slot,
    active_flags,
    normals,
    initial_gap,
    strain_operator,
    mortar,
    residual,
    jvp_one,
    jvp_two,
    field,
    halo_send,
    halo_recv,
    ghost_send,
    ghost_recv,
    request_send,
    request_recv,
    master_send,
    master_recv,
    force_send,
    force_recv,
    slave_values,
    element_values,
    master_values,
    send_sem,
    recv_sem,
    near_send_sem,
    near_recv_sem,
):
    node_count = displacement.shape[1]
    node_tiles = node_count // LANES
    slaves = slave_nodes.shape[0]
    masters = master_nodes.shape[0]
    buckets = devices * share
    group = lax.axis_index("groups")
    me = lax.axis_index("mesh") * layers + lax.axis_index("layer")

    def device(peer):
        return (group, peer // layers, lax.rem(peer, layers))

    def block(ref, peer):
        return ref.at[pl.ds(pl.multiple_of(peer * share, share), share), :]

    def far_copy(source, target, phase, k, peer, slot):
        return pltpu.make_async_remote_copy(
            src_ref=block(source, peer),
            dst_ref=block(target, slot),
            send_sem=send_sem.at[phase, k],
            recv_sem=recv_sem.at[phase, k],
            device_id=device(peer),
            device_id_type=pl.DeviceIdType.MESH,
        )

    def send(source, target, phase):
        def one(k, carry):
            far_copy(source, target, phase, k, lax.rem(me + k, devices), me).start()
            return carry

        lax.fori_loop(1, devices, one, 0)
        mine = pl.ds(pl.multiple_of(me * share, share), share)
        target[mine, :] = source[mine, :]

    def receive(source, target, phase):
        def one(k, carry):
            behind = lax.rem(me + devices - k, devices)
            far_copy(source, target, phase, k, lax.rem(me + k, devices), behind).wait_recv()
            return carry

        lax.fori_loop(1, devices, one, 0)

    def sent(source, target, phase):
        def one(k, carry):
            far_copy(source, target, phase, k, lax.rem(me + k, devices), me).wait_send()
            return carry

        lax.fori_loop(1, devices, one, 0)

    def near_copy(source, target, number, peer):
        return pltpu.make_async_remote_copy(
            src_ref=source,
            dst_ref=target,
            send_sem=near_send_sem.at[number],
            recv_sem=near_recv_sem.at[number],
            device_id=device(peer),
            device_id_type=pl.DeviceIdType.MESH,
        )

    after = lax.rem(me + 1, devices)
    before = lax.rem(me + devices - 1, devices)

    barrier = pltpu.get_barrier_semaphore()

    def greet(k, carry):
        pl.semaphore_signal(
            barrier,
            inc=1,
            device_id=device(lax.rem(me + k, devices)),
            device_id_type=pl.DeviceIdType.MESH,
        )
        return carry

    lax.fori_loop(1, devices, greet, 0)

    owner_column = pair_owner[...].astype(F32)
    first = iota((slaves, slaves), 0)
    second = iota((slaves, slaves), 1)
    owner_row = jnp.sum(jnp.where(first == second, owner_column, 0.0), axis=0, keepdims=True)
    slot_column = jnp.sum(
        jnp.where(first == second, pair_slot[...].astype(F32), 0.0), axis=1, keepdims=True
    )
    same = where01(owner_column == owner_row)
    rank_row = jnp.sum(jnp.where(first < second, same, 0.0), axis=0, keepdims=True)
    rank_column = jnp.sum(jnp.where(second < first, same, 0.0), axis=1, keepdims=True)
    bucket_row = owner_row * share + rank_row
    bucket_column = owner_column * share + rank_column
    to_bucket = where01(iota((buckets, slaves), 0).astype(F32) == bucket_row)
    normal = normals[...]
    lane = iota((slaves, LANES), 1)
    wanted = jnp.where(lane == 0, slot_column, 0.0)
    for c in range(3):
        wanted = jnp.where(lane == c + 1, normal[:, c : c + 1], wanted)
    request_send[...] = dot(to_bucket, wanted, NN)

    field[...] = jnp.zeros(field.shape, F32)
    for f, source in enumerate((displacement, tangent_one, tangent_two)):
        field[3 * f : 3 * f + 3, 0:node_count] = source[...]
    ghosts = halo_nodes.shape[1]
    halo_row = jnp.concatenate(
        [halo_nodes[...], jnp.full((1, LANES - ghosts), node_count, jnp.int32)], axis=1
    )
    halo_send[...] = lookup(
        lambda number: field[:, column(number)],
        node_tiles,
        jnp.broadcast_to(halo_row, (ROWS, LANES)),
    )

    pl.semaphore_wait(barrier, devices - 1)
    send(request_send, request_recv, 0)
    near_copy(halo_send, halo_recv, 0, before).start()

    def nodal(index, fc):
        return lookup(lambda number: field[fc : fc + 1, column(number)], node_tiles, index)

    master_index = master_nodes[...]
    parts = [thirds(nodal(master_index, fc)) for fc in range(9)]
    served = jnp.concatenate(
        [jnp.concatenate([part[k] for part in parts], axis=1) for k in range(3)], axis=0
    )
    receive(request_send, request_recv, 0)
    request = request_recv[...]
    slot = request[:, 0:1]
    pick = where01(
        lax.rem(iota((buckets, 3 * masters), 1), masters).astype(F32) == slot
    ).astype(BF16)
    chosen = dot16(pick, served, NN)
    for f in range(FIELDS):
        value = request[:, 1:2] * chosen[:, column(3 * f)]
        for c in range(1, 3):
            value = value + request[:, c + 1 : c + 2] * chosen[:, column(3 * f + c)]
        master_send[:, column(f)] = value
    send(master_send, master_recv, 1)

    slave_index = slave_nodes[...]
    slave_normal = []
    for f in range(FIELDS):
        value = normal[:, 0:1] * nodal(slave_index, 3 * f)
        for c in range(1, 3):
            value = value + normal[:, c : c + 1] * nodal(slave_index, 3 * f + c)
        slave_normal.append(value)
    live = jnp.where(slave_index < node_count, PENALTY, 0.0)
    weight = active_flags[...].astype(F32) * live

    near_copy(halo_send, halo_recv, 0, before).wait_recv()
    field[:, node_count : node_count + LANES] = halo_recv[...]
    corner = connectivity[...]
    elements = jnp.concatenate(
        [
            jnp.concatenate(
                [
                    lookup(
                        lambda number: field[3 * f + c : 3 * f + c + 1, column(number)],
                        node_tiles + 1,
                        corner,
                    )
                    for c in range(3)
                ],
                axis=0,
            )
            for f in range(FIELDS)
        ],
        axis=1,
    )
    entries = strain_operator.shape[1]
    order = iota((entries, entries), 1)
    operator = dot(
        strain_operator[...],
        where01(iota((entries, entries), 0) == 3 * lax.rem(order, 8) + order // 8),
        NN,
    )
    strain = dot(operator, elements, NN)
    scale = element_scale[...]
    base = strain[:, 0:LANES]
    hyperbolic = jnp.tanh(base)
    stiffness = scale * (1.0 + 0.5 * (1.0 - hyperbolic * hyperbolic))
    stress = jnp.concatenate(
        [
            scale * (base + 0.5 * hyperbolic),
            stiffness * strain[:, column(1)],
            stiffness * strain[:, column(2)],
        ],
        axis=1,
    )
    element_force = dot(operator, stress, TN)
    element_values[...] = jnp.zeros(element_values.shape, F32)
    for f in range(FIELDS):
        for c in range(3):
            element_values[:, 3 * f + c, :] = element_force[8 * c : 8 * c + 8, column(f)]
    total = jnp.zeros((2 * ROWS * (node_tiles + 1), LANES), F32)
    total = add_rows(element_values, connectivity, 0, 1, node_tiles + 1, total)
    ghost_send[...] = tile_sum(total, node_tiles)
    near_copy(ghost_send, ghost_recv, 1, after).start()
    total = total[: 2 * ROWS * node_tiles]

    receive(master_send, master_recv, 1)
    from_bucket = where01(iota((slaves, buckets), 1).astype(F32) == bucket_column).astype(BF16)
    top, rest = halves(master_recv[...])
    fetched = dot16(from_bucket, top, NN) + dot16(from_bucket, rest, NN)
    fetched = jnp.concatenate([fetched[:, column(f)] for f in range(FIELDS)], axis=0)
    projected = dot(fetched, mortar[...], NT)
    change = [slave_normal[f] - projected[column(f, slaves)] for f in range(FIELDS)]
    closing = -(initial_gap[...] + change[0])
    small = jnp.exp(-jnp.abs(closing))
    slope = -weight * jnp.where(closing >= 0.0, 1.0, small) / (1.0 + small)
    multiplier = [
        weight * (jnp.maximum(closing, 0.0) + jnp.log1p(small)),
        slope * change[1],
        slope * change[2],
    ]
    spread = dot(jnp.concatenate(multiplier, axis=0), mortar[...], NN)
    spread = jnp.concatenate([spread[column(f, slaves)] for f in range(FIELDS)], axis=1)
    top, rest = halves(spread)
    to_bucket = to_bucket.astype(BF16)
    force_send[...] = dot16(to_bucket, top, NN) + dot16(to_bucket, rest, NN)
    send(force_send, force_recv, 2)

    slave_values[...] = jnp.zeros(slave_values.shape, F32)
    for f in range(FIELDS):
        for c in range(3):
            slave_values[:, 3 * f + c, :] = -normal[:, c : c + 1] * multiplier[f]
    total = add_rows(slave_values, slave_nodes, 0, slaves // 8, node_tiles, total)

    near_copy(ghost_send, ghost_recv, 1, after).wait_recv()
    left, right = add_operands(ghost_recv[...], halo_row, node_tiles)
    total = total + dot16(left, right, NT)

    master_values[...] = jnp.zeros(master_values.shape, F32)
    at_slot = jnp.transpose(request, (1, 0))[0:1, :]
    to_slot = where01(iota((masters, buckets), 0).astype(F32) == at_slot).astype(BF16)
    receive(force_send, force_recv, 2)
    for f in range(FIELDS):
        arrived = force_recv[:, column(f)]
        for c in range(3):
            top, rest = halves(request[:, c + 1 : c + 2] * arrived)
            master_values[:, 3 * f + c, :] = dot16(to_slot, top, NN) + dot16(to_slot, rest, NN)
    total = add_rows(master_values, master_nodes, 0, masters // 8, node_tiles, total)
    for number in range(node_tiles):
        value = tile_sum(total, number)
        residual[:, column(number)] = value[0:3] - external_force[:, column(number)]
        jvp_one[:, column(number)] = value[3:6]
        jvp_two[:, column(number)] = value[6:9]

    sent(request_send, request_recv, 0)
    sent(master_send, master_recv, 1)
    sent(force_send, force_recv, 2)
    near_copy(halo_send, halo_recv, 0, before).wait_send()
    near_copy(ghost_send, ghost_recv, 1, after).wait_send()


def on_device(*arguments):
    arguments = list(arguments)
    displacement, slave_nodes, master_nodes = arguments[0], arguments[7], arguments[8]
    arguments[5] = arguments[5].reshape(1, -1)
    arguments[6] = arguments[6].reshape(1, -1)
    arguments[10] = arguments[10].reshape(1, -1)
    node_count = displacement.shape[1]
    slaves, masters = slave_nodes.shape[0], master_nodes.shape[0]
    corners = arguments[4].shape[0]
    layers = lax.axis_size("layer")
    devices = lax.axis_size("mesh") * layers
    capacity = max(2, 2 * slaves // devices)
    share = -(-capacity // 8) * 8
    buckets = devices * share
    vmem = lambda *shape: pltpu.VMEM(shape, F32)
    near = vmem(ROWS, LANES)
    wide = vmem(buckets, FIELDS * LANES)
    narrow = vmem(buckets, LANES)
    result = jax.ShapeDtypeStruct((3, node_count), F32)
    return pl.pallas_call(
        functools.partial(kernel, devices, layers, share),
        out_shape=(result, result, result),
        in_specs=[pl.BlockSpec(memory_space=pltpu.VMEM)] * len(arguments),
        out_specs=tuple([pl.BlockSpec(memory_space=pltpu.VMEM)] * 3),
        scratch_shapes=[
            vmem(ROWS, node_count + LANES),
            near,
            near,
            near,
            near,
            narrow,
            narrow,
            wide,
            wide,
            wide,
            wide,
            vmem(slaves, ROWS, LANES),
            vmem(corners, ROWS, LANES),
            vmem(masters, ROWS, LANES),
            pltpu.SemaphoreType.DMA((3, devices)),
            pltpu.SemaphoreType.DMA((3, devices)),
            pltpu.SemaphoreType.DMA((2,)),
            pltpu.SemaphoreType.DMA((2,)),
        ],
        compiler_params=pltpu.CompilerParams(
            collective_id=0, has_side_effects=True, vmem_limit_bytes=40 * 1024 * 1024
        ),
    )(*arguments)


def solution(mesh):
    split = ("groups", "mesh", "layer")
    wide, flat, tall = P(None, split), P(split), P(split, None)
    return jax.shard_map(
        on_device,
        mesh=mesh,
        in_specs=(wide,) * 5 + (flat, flat) + (tall,) * 3 + (flat,) + (tall,) * 3 + (P(), P()),
        out_specs=(wide, wide, wide),
        check_vma=False,
    )
```

```python
import functools

import jax
import jax.numpy as jnp
from jax import lax
from jax.experimental import pallas as pl
from jax.experimental.pallas import tpu as pltpu
from jax.sharding import PartitionSpec as P

PENALTY = 2.0
HIGH = lax.Precision.HIGHEST
LANES = 128
ROWS = 16
FIELDS = 3
NN = ((1,), (0,))
NT = ((1,), (1,))
TN = ((0,), (0,))
LOAD_ORDER = (9, 10, 12, 0, 1, 2, 6, 8, 7, 4, 5, 14, 11, 13, 15, 3)
F32 = jnp.float32
BF16 = jnp.bfloat16


def dot(left, right, dims):
    return lax.dot_general(
        left, right, (dims, ((), ())), precision=HIGH, preferred_element_type=F32
    )


def dot16(left, right, dims):
    return lax.dot_general(left, right, (dims, ((), ())), preferred_element_type=F32)


def halves(value):
    top = value.astype(BF16)
    return top, (value - top.astype(F32)).astype(BF16)


def thirds(value):
    top = value.astype(BF16)
    rest = value - top.astype(F32)
    middle = rest.astype(BF16)
    return top, middle, (rest - middle.astype(F32)).astype(BF16)


def iota(shape, dim):
    return lax.broadcasted_iota(jnp.int32, shape, dim)


def where01(mask):
    return jnp.where(mask, 1.0, 0.0).astype(F32)


def column(index, by=LANES):
    return slice(index * by, (index + 1) * by)


def lookup(tile_of, tiles, index):
    lane = jnp.bitwise_and(index, LANES - 1)
    tile = jnp.right_shift(index, 7)
    found = jnp.zeros(index.shape, F32)
    for number in range(tiles):
        table = jnp.broadcast_to(tile_of(number), index.shape)
        picked = jnp.take_along_axis(table, lane, axis=1, mode="promise_in_bounds")
        found = jnp.where(tile == number, picked, found)
    return found


def add_operands(values, index, tiles):
    lane = jnp.bitwise_and(index, LANES - 1)
    tile = jnp.right_shift(index, 7)
    top = values.astype(BF16).astype(F32)
    both = jnp.concatenate([top, values - top], axis=0)
    left = jnp.concatenate(
        [jnp.where(tile == number, both, 0.0).astype(BF16) for number in range(tiles)], axis=0
    )
    right = where01(lane == iota((LANES, LANES), 0)).astype(BF16)
    return left, right


def add_rows(value_ref, index_ref, first, groups, tiles, total):
    def step(group, total):
        rows = index_ref[pl.ds(pl.multiple_of(group * 8, 8), 8), :]
        pairs = [
            add_operands(value_ref[first + group * 8 + k], rows[k : k + 1, :], tiles)
            for k in range(8)
        ]
        left = jnp.concatenate([pair[0] for pair in pairs], axis=1)
        right = jnp.concatenate([pair[1] for pair in pairs], axis=1)
        return total + dot16(left, right, NT)

    return lax.fori_loop(0, groups, step, total)


def tile_sum(total, number):
    start = number * 2 * ROWS
    return total[start : start + ROWS] + total[start + ROWS : start + 2 * ROWS]


def kernel(
    devices,
    layers,
    share,
    *refs,
):
    sources, outputs, held, scratch = refs[:16], refs[16:19], refs[19:35], refs[35:]
    (
        displacement,
        tangent_one,
        tangent_two,
        external_force,
        connectivity,
        element_scale,
        halo_nodes,
        slave_nodes,
        master_nodes,
        pair_owner,
        pair_slot,
        active_flags,
        normals,
        initial_gap,
        strain_operator,
        mortar,
    ) = held
    residual, jvp_one, jvp_two = outputs
    (
        field,
        halo_send,
        halo_recv,
        ghost_send,
        ghost_recv,
        request_send,
        request_recv,
        master_send,
        master_recv,
        force_send,
        force_recv,
        slave_values,
        element_values,
        master_values,
        send_sem,
        recv_sem,
        near_send_sem,
        near_recv_sem,
        input_sem,
    ) = scratch
    node_count = displacement.shape[1]
    node_tiles = node_count // LANES
    slaves = slave_nodes.shape[0]
    masters = master_nodes.shape[0]
    buckets = devices * share
    group = lax.axis_index("groups")
    me = lax.axis_index("mesh") * layers + lax.axis_index("layer")

    def device(peer):
        return (group, peer // layers, lax.rem(peer, layers))

    def block(ref, peer):
        return ref.at[pl.ds(pl.multiple_of(peer * share, share), share), :]

    def far_copy(source, target, phase, k, peer, slot):
        return pltpu.make_async_remote_copy(
            src_ref=block(source, peer),
            dst_ref=block(target, slot),
            send_sem=send_sem.at[phase, k],
            recv_sem=recv_sem.at[phase, k],
            device_id=device(peer),
            device_id_type=pl.DeviceIdType.MESH,
        )

    def send(source, target, phase):
        def one(k, carry):
            far_copy(source, target, phase, k, lax.rem(me + k, devices), me).start()
            return carry

        lax.fori_loop(1, devices, one, 0)
        mine = pl.ds(pl.multiple_of(me * share, share), share)
        target[mine, :] = source[mine, :]

    def receive(source, target, phase):
        def one(k, carry):
            behind = lax.rem(me + devices - k, devices)
            far_copy(source, target, phase, k, lax.rem(me + k, devices), behind).wait_recv()
            return carry

        lax.fori_loop(1, devices, one, 0)

    def sent(source, target, phase):
        def one(k, carry):
            far_copy(source, target, phase, k, lax.rem(me + k, devices), me).wait_send()
            return carry

        lax.fori_loop(1, devices, one, 0)

    def near_copy(source, target, number, peer):
        return pltpu.make_async_remote_copy(
            src_ref=source,
            dst_ref=target,
            send_sem=near_send_sem.at[number],
            recv_sem=near_recv_sem.at[number],
            device_id=device(peer),
            device_id_type=pl.DeviceIdType.MESH,
        )

    after = lax.rem(me + 1, devices)
    before = lax.rem(me + devices - 1, devices)

    loads = [
        pltpu.make_async_copy(source, target, input_sem.at[number])
        for number, source, target in zip(range(len(sources)), sources, held)
    ]
    for number in LOAD_ORDER:
        loads[number].start()

    def ready(*numbers):
        for number in numbers:
            loads[number].wait()

    barrier = pltpu.get_barrier_semaphore()

    def greet(k, carry):
        pl.semaphore_signal(
            barrier,
            inc=1,
            device_id=device(lax.rem(me + k, devices)),
            device_id_type=pl.DeviceIdType.MESH,
        )
        return carry

    lax.fori_loop(1, devices, greet, 0)

    ready(9, 10, 12)
    first = iota((slaves, slaves), 0)
    second = iota((slaves, slaves), 1)

    def stand(row):
        return jnp.sum(jnp.where(first == second, row, 0.0), axis=1, keepdims=True)

    owner_row = pair_owner[...].astype(F32)
    owner_column = stand(owner_row)
    slot_column = stand(pair_slot[...].astype(F32))
    normal = [stand(normals[c : c + 1, :]) for c in range(3)]
    same = where01(owner_column == owner_row)
    rank_row = jnp.sum(jnp.where(first < second, same, 0.0), axis=0, keepdims=True)
    rank_column = jnp.sum(jnp.where(second < first, same, 0.0), axis=1, keepdims=True)
    bucket_row = owner_row * share + rank_row
    bucket_column = owner_column * share + rank_column
    to_bucket = where01(iota((buckets, slaves), 0).astype(F32) == bucket_row)
    lane = iota((slaves, LANES), 1)
    wanted = jnp.where(lane == 0, slot_column, 0.0)
    for c in range(3):
        wanted = jnp.where(lane == c + 1, normal[c], wanted)
    request_send[...] = dot(to_bucket, wanted, NN)

    field[...] = jnp.zeros(field.shape, F32)
    ready(0, 1, 2, 6)
    for f, source in enumerate((displacement, tangent_one, tangent_two)):
        field[3 * f : 3 * f + 3, 0:node_count] = source[...]
    ghosts = halo_nodes.shape[1]
    halo_row = jnp.concatenate(
        [halo_nodes[...], jnp.full((1, LANES - ghosts), node_count, jnp.int32)], axis=1
    )
    halo_send[...] = lookup(
        lambda number: field[:, column(number)],
        node_tiles,
        jnp.broadcast_to(halo_row, (ROWS, LANES)),
    )

    pl.semaphore_wait(barrier, devices - 1)
    send(request_send, request_recv, 0)
    near_copy(halo_send, halo_recv, 0, before).start()

    def nodal(index, fc):
        return lookup(lambda number: field[fc : fc + 1, column(number)], node_tiles, index)

    ready(8)
    master_index = master_nodes[...]
    parts = [thirds(nodal(master_index, fc)) for fc in range(9)]
    served = jnp.concatenate(
        [jnp.concatenate([part[k] for part in parts], axis=1) for k in range(3)], axis=0
    )
    receive(request_send, request_recv, 0)
    request = request_recv[...]
    slot = request[:, 0:1]
    pick = where01(
        lax.rem(iota((buckets, 3 * masters), 1), masters).astype(F32) == slot
    ).astype(BF16)
    chosen = dot16(pick, served, NN)
    for f in range(FIELDS):
        value = request[:, 1:2] * chosen[:, column(3 * f)]
        for c in range(1, 3):
            value = value + request[:, c + 1 : c + 2] * chosen[:, column(3 * f + c)]
        master_send[:, column(f)] = value
    send(master_send, master_recv, 1)

    ready(7)
    slave_index = slave_nodes[...]
    slave_normal = []
    for f in range(FIELDS):
        value = normal[0] * nodal(slave_index, 3 * f)
        for c in range(1, 3):
            value = value + normal[c] * nodal(slave_index, 3 * f + c)
        slave_normal.append(value)
    live = jnp.where(slave_index < node_count, PENALTY, 0.0)
    ready(11)
    weight = active_flags[...].astype(F32) * live

    ready(4, 5, 14)
    near_copy(halo_send, halo_recv, 0, before).wait_recv()
    field[:, node_count : node_count + LANES] = halo_recv[...]
    corner = connectivity[...]
    elements = jnp.concatenate(
        [
            jnp.concatenate(
                [
                    lookup(
                        lambda number: field[3 * f + c : 3 * f + c + 1, column(number)],
                        node_tiles + 1,
                        corner,
                    )
                    for c in range(3)
                ],
                axis=0,
            )
            for f in range(FIELDS)
        ],
        axis=1,
    )
    entries = strain_operator.shape[0]
    order = iota((entries, entries), 0)
    operator = dot(
        where01(iota((entries, entries), 1) == 3 * lax.rem(order, 8) + order // 8),
        strain_operator[...],
        NN,
    )
    strain = dot(operator, elements, TN)
    scale = element_scale[...]
    base = strain[:, 0:LANES]
    hyperbolic = jnp.tanh(base)
    stiffness = scale * (1.0 + 0.5 * (1.0 - hyperbolic * hyperbolic))
    stress = jnp.concatenate(
        [
            scale * (base + 0.5 * hyperbolic),
            stiffness * strain[:, column(1)],
            stiffness * strain[:, column(2)],
        ],
        axis=1,
    )
    element_force = dot(operator, stress, NN)
    element_values[...] = jnp.zeros(element_values.shape, F32)
    for f in range(FIELDS):
        for c in range(3):
            element_values[:, 3 * f + c, :] = element_force[8 * c : 8 * c + 8, column(f)]
    total = jnp.zeros((2 * ROWS * (node_tiles + 1), LANES), F32)
    total = add_rows(element_values, connectivity, 0, 1, node_tiles + 1, total)
    ghost_send[...] = tile_sum(total, node_tiles)
    near_copy(ghost_send, ghost_recv, 1, after).start()
    total = total[: 2 * ROWS * node_tiles]

    ready(13, 15, 3)
    receive(master_send, master_recv, 1)
    from_bucket = where01(iota((slaves, buckets), 1).astype(F32) == bucket_column).astype(BF16)
    top, rest = halves(master_recv[...])
    fetched = dot16(from_bucket, top, NN) + dot16(from_bucket, rest, NN)
    fetched = jnp.concatenate([fetched[:, column(f)] for f in range(FIELDS)], axis=0)
    projected = dot(fetched, mortar[...], NT)
    change = [slave_normal[f] - projected[column(f, slaves)] for f in range(FIELDS)]
    closing = -(initial_gap[...] + change[0])
    small = jnp.exp(-jnp.abs(closing))
    slope = -weight * jnp.where(closing >= 0.0, 1.0, small) / (1.0 + small)
    multiplier = [
        weight * (jnp.maximum(closing, 0.0) + jnp.log1p(small)),
        slope * change[1],
        slope * change[2],
    ]
    spread = dot(jnp.concatenate(multiplier, axis=0), mortar[...], NN)
    spread = jnp.concatenate([spread[column(f, slaves)] for f in range(FIELDS)], axis=1)
    top, rest = halves(spread)
    to_bucket = to_bucket.astype(BF16)
    force_send[...] = dot16(to_bucket, top, NN) + dot16(to_bucket, rest, NN)
    send(force_send, force_recv, 2)

    slave_values[...] = jnp.zeros(slave_values.shape, F32)
    for f in range(FIELDS):
        for c in range(3):
            slave_values[:, 3 * f + c, :] = -normal[c] * multiplier[f]
    total = add_rows(slave_values, slave_nodes, 0, slaves // 8, node_tiles, total)

    near_copy(ghost_send, ghost_recv, 1, after).wait_recv()
    left, right = add_operands(ghost_recv[...], halo_row, node_tiles)
    total = total + dot16(left, right, NT)

    master_values[...] = jnp.zeros(master_values.shape, F32)
    at_slot = jnp.transpose(request, (1, 0))[0:1, :]
    to_slot = where01(iota((masters, buckets), 0).astype(F32) == at_slot).astype(BF16)
    receive(force_send, force_recv, 2)
    for f in range(FIELDS):
        arrived = force_recv[:, column(f)]
        for c in range(3):
            top, rest = halves(request[:, c + 1 : c + 2] * arrived)
            master_values[:, 3 * f + c, :] = dot16(to_slot, top, NN) + dot16(to_slot, rest, NN)
    total = add_rows(master_values, master_nodes, 0, masters // 8, node_tiles, total)
    for number in range(node_tiles):
        value = tile_sum(total, number)
        residual[:, column(number)] = value[0:3] - external_force[:, column(number)]
        jvp_one[:, column(number)] = value[3:6]
        jvp_two[:, column(number)] = value[6:9]

    sent(request_send, request_recv, 0)
    sent(master_send, master_recv, 1)
    sent(force_send, force_recv, 2)
    near_copy(halo_send, halo_recv, 0, before).wait_send()
    near_copy(ghost_send, ghost_recv, 1, after).wait_send()


def on_device(*arguments):
    arguments = list(arguments)
    displacement, slave_nodes, master_nodes = arguments[0], arguments[7], arguments[8]
    arguments[5] = arguments[5].reshape(1, -1)
    arguments[6] = arguments[6].reshape(1, -1)
    arguments[9] = arguments[9].T
    arguments[10] = arguments[10].reshape(1, -1)
    arguments[12] = arguments[12].T
    arguments[14] = arguments[14].T
    node_count = displacement.shape[1]
    slaves, masters = slave_nodes.shape[0], master_nodes.shape[0]
    corners = arguments[4].shape[0]
    layers = lax.axis_size("layer")
    devices = lax.axis_size("mesh") * layers
    capacity = max(2, 2 * slaves // devices)
    share = -(-capacity // 8) * 8
    buckets = devices * share
    vmem = lambda *shape: pltpu.VMEM(shape, F32)
    near = vmem(ROWS, LANES)
    wide = vmem(buckets, FIELDS * LANES)
    narrow = vmem(buckets, LANES)
    result = jax.ShapeDtypeStruct((3, node_count), F32)
    return pl.pallas_call(
        functools.partial(kernel, devices, layers, share),
        out_shape=(result, result, result),
        in_specs=[pl.BlockSpec(memory_space=pltpu.HBM)] * len(arguments),
        out_specs=tuple([pl.BlockSpec(memory_space=pltpu.VMEM)] * 3),
        scratch_shapes=[pltpu.VMEM(each.shape, each.dtype) for each in arguments]
        + [
            vmem(ROWS, node_count + LANES),
            near,
            near,
            near,
            near,
            narrow,
            narrow,
            wide,
            wide,
            wide,
            wide,
            vmem(slaves, ROWS, LANES),
            vmem(corners, ROWS, LANES),
            vmem(masters, ROWS, LANES),
            pltpu.SemaphoreType.DMA((3, devices)),
            pltpu.SemaphoreType.DMA((3, devices)),
            pltpu.SemaphoreType.DMA((2,)),
            pltpu.SemaphoreType.DMA((2,)),
            pltpu.SemaphoreType.DMA((len(arguments),)),
        ],
        compiler_params=pltpu.CompilerParams(
            collective_id=0, has_side_effects=True, vmem_limit_bytes=63 * 1024 * 1024
        ),
    )(*arguments)


def solution(mesh):
    split = ("groups", "mesh", "layer")
    wide, flat, tall = P(None, split), P(split), P(split, None)
    return jax.shard_map(
        on_device,
        mesh=mesh,
        in_specs=(wide,) * 5 + (flat, flat) + (tall,) * 3 + (flat,) + (tall,) * 3 + (P(), P()),
        out_specs=(wide, wide, wide),
        check_vma=False,
    )
```

```python
import functools

import jax
import jax.numpy as jnp
from jax import lax
from jax.experimental import pallas as pl
from jax.experimental.pallas import tpu as pltpu
from jax.sharding import PartitionSpec as P

PENALTY = 2.0
HIGH = lax.Precision.HIGHEST
LANES = 128
ROWS = 16
FIELDS = 3
PHASES = 1 + 2 * FIELDS
NN = ((1,), (0,))
NT = ((1,), (1,))
TN = ((0,), (0,))
LOAD_ORDER = (9, 10, 12, 0, 1, 2, 6, 8, 7, 4, 5, 14, 11, 13, 15, 3)
F32 = jnp.float32
BF16 = jnp.bfloat16


def dot(left, right, dims):
    return lax.dot_general(
        left, right, (dims, ((), ())), precision=HIGH, preferred_element_type=F32
    )


def dot16(left, right, dims):
    return lax.dot_general(left, right, (dims, ((), ())), preferred_element_type=F32)


def halves(value):
    top = value.astype(BF16)
    return top, (value - top.astype(F32)).astype(BF16)


def thirds(value):
    top = value.astype(BF16)
    rest = value - top.astype(F32)
    middle = rest.astype(BF16)
    return top, middle, (rest - middle.astype(F32)).astype(BF16)


def iota(shape, dim):
    return lax.broadcasted_iota(jnp.int32, shape, dim)


def where01(mask):
    return jnp.where(mask, 1.0, 0.0).astype(F32)


def column(index, by=LANES):
    return slice(index * by, (index + 1) * by)


def lookup(tile_of, tiles, index):
    lane = jnp.bitwise_and(index, LANES - 1)
    tile = jnp.right_shift(index, 7)
    found = jnp.zeros(index.shape, F32)
    for number in range(tiles):
        table = jnp.broadcast_to(tile_of(number), index.shape)
        picked = jnp.take_along_axis(table, lane, axis=1, mode="promise_in_bounds")
        found = jnp.where(tile == number, picked, found)
    return found


def left_operand(values, index, tiles):
    tile = jnp.right_shift(index, 7)
    top = values.astype(BF16).astype(F32)
    both = jnp.concatenate([top, values - top], axis=0)
    return jnp.concatenate(
        [jnp.where(tile == number, both, 0.0).astype(BF16) for number in range(tiles)], axis=0
    )


def right_operand(index):
    lane = jnp.bitwise_and(index, LANES - 1)
    return where01(lane == iota((LANES, LANES), 0)).astype(BF16)


def eight_rows(index_ref, group):
    return index_ref[pl.ds(pl.multiple_of(group * 8, 8), 8), :]


def fill_right(right_ref, index_ref, groups):
    def step(group, carry):
        rows = eight_rows(index_ref, group)
        for k in range(8):
            right_ref[group, :, column(k)] = right_operand(rows[k : k + 1, :])
        return carry

    lax.fori_loop(0, groups, step, 0)


def add_rows(value_ref, index_ref, right_ref, groups, tiles, total):
    def step(group, total):
        rows = eight_rows(index_ref, group)
        left = [left_operand(value_ref[group * 8 + k], rows[k : k + 1, :], tiles) for k in range(8)]
        return total + dot16(jnp.concatenate(left, axis=1), right_ref[group], NT)

    return lax.fori_loop(0, groups, step, total)


def three_products(value, factor, dims):
    top, rest = halves(value)
    return dot16(jnp.concatenate([top, top, rest], axis=1), factor, dims)


def tile_sum(total, number):
    start = number * 2 * ROWS
    return total[start : start + ROWS] + total[start + ROWS : start + 2 * ROWS]


def kernel(
    devices,
    layers,
    share,
    *refs,
):
    sources, outputs, held, scratch = refs[:16], refs[16:17], refs[17:33], refs[33:]
    (
        displacement,
        tangent_one,
        tangent_two,
        external_force,
        connectivity,
        element_scale,
        halo_nodes,
        slave_nodes,
        master_nodes,
        pair_owner,
        pair_slot,
        active_flags,
        normals,
        initial_gap,
        strain_operator,
        mortar,
    ) = held
    (result,) = outputs
    (
        field,
        halo_send,
        halo_recv,
        ghost_send,
        ghost_recv,
        outbox,
        inbox,
        slave_values,
        element_values,
        master_values,
        slave_right,
        element_right,
        master_right,
        send_sem,
        recv_sem,
        near_send_sem,
        near_recv_sem,
        input_sem,
    ) = scratch
    node_count = displacement.shape[1]
    node_tiles = node_count // LANES
    slaves = slave_nodes.shape[0]
    masters = master_nodes.shape[0]
    buckets = devices * share
    group = lax.axis_index("groups")
    me = lax.axis_index("mesh") * layers + lax.axis_index("layer")

    after = lax.rem(me + 1, devices)
    before = lax.rem(me + devices - 1, devices)

    def device(peer):
        return (group, peer // layers, lax.rem(peer, layers))

    def block(ref, phase, peer):
        return ref.at[phase, pl.ds(pl.multiple_of(peer * share, share), share), :]

    def send(phase):
        def one(k, carry):
            peer = lax.rem(me + k, devices)
            pltpu.make_async_remote_copy(
                src_ref=block(outbox, phase, peer),
                dst_ref=block(inbox, phase, me),
                send_sem=send_sem.at[phase],
                recv_sem=recv_sem.at[phase],
                device_id=device(peer),
                device_id_type=pl.DeviceIdType.MESH,
            ).start()
            return carry

        lax.fori_loop(1, devices, one, 0)
        mine = pl.ds(pl.multiple_of(me * share, share), share)
        inbox[phase, mine, :] = outbox[phase, mine, :]

    def whole(phase):
        rows = pl.ds(0, buckets - share)
        return pltpu.make_async_remote_copy(
            src_ref=outbox.at[phase, rows, :],
            dst_ref=inbox.at[phase, rows, :],
            send_sem=send_sem.at[phase],
            recv_sem=recv_sem.at[phase],
            device_id=device(after),
            device_id_type=pl.DeviceIdType.MESH,
        )

    def receive(phase):
        whole(phase).wait_recv()

    def sent(phase):
        whole(phase).wait_send()

    def near_copy(source, target, number, peer):
        return pltpu.make_async_remote_copy(
            src_ref=source,
            dst_ref=target,
            send_sem=near_send_sem.at[number],
            recv_sem=near_recv_sem.at[number],
            device_id=device(peer),
            device_id_type=pl.DeviceIdType.MESH,
        )

    barrier = pltpu.get_barrier_semaphore()

    def greet(k, carry):
        pl.semaphore_signal(
            barrier,
            inc=1,
            device_id=device(lax.rem(me + k, devices)),
            device_id_type=pl.DeviceIdType.MESH,
        )
        return carry

    lax.fori_loop(1, devices, greet, 0)

    loads = [
        pltpu.make_async_copy(source, target, input_sem.at[number])
        for number, source, target in zip(range(len(sources)), sources, held)
    ]
    for number in LOAD_ORDER:
        loads[number].start()

    def ready(*numbers):
        for number in numbers:
            loads[number].wait()

    ready(9, 10, 12)
    first = iota((slaves, slaves), 0)
    second = iota((slaves, slaves), 1)

    def stand(row):
        return jnp.sum(jnp.where(first == second, row, 0.0), axis=1, keepdims=True)

    owner_row = pair_owner[...].astype(F32)
    owner_column = stand(owner_row)
    slot_column = stand(pair_slot[...].astype(F32))
    normal = [stand(normals[c : c + 1, :]) for c in range(3)]
    same = where01(owner_column == owner_row)
    rank_row = jnp.sum(jnp.where(first < second, same, 0.0), axis=0, keepdims=True)
    rank_column = jnp.sum(jnp.where(second < first, same, 0.0), axis=1, keepdims=True)
    bucket_row = owner_row * share + rank_row
    bucket_column = owner_column * share + rank_column
    to_bucket = where01(iota((buckets, slaves), 0).astype(F32) == bucket_row)
    lane = iota((slaves, LANES), 1)
    wanted = jnp.where(lane == 0, slot_column, 0.0)
    for c in range(3):
        wanted = jnp.where(lane == c + 1, normal[c], wanted)
    outbox[0] = dot(to_bucket, wanted, NN)

    field[...] = jnp.zeros(field.shape, F32)
    ready(0, 1, 2, 6)
    for f, source in enumerate((displacement, tangent_one, tangent_two)):
        field[3 * f : 3 * f + 3, 0:node_count] = source[...]
    ghosts = halo_nodes.shape[1]
    halo_row = jnp.concatenate(
        [halo_nodes[...], jnp.full((1, LANES - ghosts), node_count, jnp.int32)], axis=1
    )
    halo_send[...] = lookup(
        lambda number: field[:, column(number)],
        node_tiles,
        jnp.broadcast_to(halo_row, (ROWS, LANES)),
    )


    def nodal(index, fc):
        return lookup(lambda number: field[fc : fc + 1, column(number)], node_tiles, index)

    ready(8)
    master_index = master_nodes[...]
    parts = [thirds(nodal(master_index, fc)) for fc in range(9)]
    served = jnp.concatenate(
        [jnp.concatenate([part[k] for part in parts], axis=1) for k in range(3)], axis=0
    )
    ready(7)
    slave_index = slave_nodes[...]
    slave_normal = []
    for f in range(FIELDS):
        value = normal[0] * nodal(slave_index, 3 * f)
        for c in range(1, 3):
            value = value + normal[c] * nodal(slave_index, 3 * f + c)
        slave_normal.append(value)

    pl.semaphore_wait(barrier, devices - 1)
    send(0)
    near_copy(halo_send, halo_recv, 0, before).start()

    ready(4, 5, 11, 13, 14, 15, 3)
    live = jnp.where(slave_index < node_count, PENALTY, 0.0)
    weight = active_flags[...].astype(F32) * live
    top, rest = halves(mortar[...])
    mortar_rows = jnp.concatenate([top, rest, top], axis=0)
    mortar_columns = jnp.concatenate([top, rest, top], axis=1)
    fill_right(slave_right, slave_nodes, slaves // 8)
    fill_right(element_right, connectivity, 1)
    fill_right(master_right, master_nodes, masters // 8)

    receive(0)
    request = inbox[0]
    pick = where01(
        lax.rem(iota((buckets, 3 * masters), 1), masters).astype(F32) == request[:, 0:1]
    ).astype(BF16)
    for f in range(FIELDS):
        chosen = dot16(pick, served[:, column(f, 3 * LANES)], NN)
        value = request[:, 1:2] * chosen[:, column(0)]
        for c in range(1, 3):
            value = value + request[:, c + 1 : c + 2] * chosen[:, column(c)]
        outbox[1 + f] = value
        send(1 + f)

    near_copy(halo_send, halo_recv, 0, before).wait_recv()
    field[:, node_count : node_count + LANES] = halo_recv[...]
    corner = connectivity[...]
    elements = jnp.concatenate(
        [
            jnp.concatenate(
                [
                    lookup(
                        lambda number: field[3 * f + c : 3 * f + c + 1, column(number)],
                        node_tiles + 1,
                        corner,
                    )
                    for c in range(3)
                ],
                axis=0,
            )
            for f in range(FIELDS)
        ],
        axis=1,
    )
    entries = strain_operator.shape[0]
    order = iota((entries, entries), 0)
    operator = dot(
        where01(iota((entries, entries), 1) == 3 * lax.rem(order, 8) + order // 8),
        strain_operator[...],
        NN,
    )
    strain = dot(operator, elements, TN)
    scale = element_scale[...]
    base = strain[:, 0:LANES]
    hyperbolic = jnp.tanh(base)
    stiffness = scale * (1.0 + 0.5 * (1.0 - hyperbolic * hyperbolic))
    stress = jnp.concatenate(
        [
            scale * (base + 0.5 * hyperbolic),
            stiffness * strain[:, column(1)],
            stiffness * strain[:, column(2)],
        ],
        axis=1,
    )
    element_force = dot(operator, stress, NN)
    element_values[...] = jnp.zeros(element_values.shape, F32)
    for f in range(FIELDS):
        for c in range(3):
            element_values[:, 3 * f + c, :] = element_force[8 * c : 8 * c + 8, column(f)]
    total = jnp.zeros((2 * ROWS * (node_tiles + 1), LANES), F32)
    total = add_rows(element_values, connectivity, element_right, 1, node_tiles + 1, total)
    ghost_send[...] = tile_sum(total, node_tiles)
    near_copy(ghost_send, ghost_recv, 1, after).start()
    total = total[: 2 * ROWS * node_tiles]

    from_bucket = where01(iota((slaves, buckets), 1).astype(F32) == bucket_column).astype(BF16)
    to_bucket = to_bucket.astype(BF16)
    multiplier = []
    slope = None
    for f in range(FIELDS):
        receive(1 + f)
        top, rest = halves(inbox[1 + f])
        fetched = dot16(from_bucket, top, NN) + dot16(from_bucket, rest, NN)
        change = slave_normal[f] - three_products(fetched, mortar_columns, NT)
        if f == 0:
            closing = -(initial_gap[...] + change)
            small = jnp.exp(-jnp.abs(closing))
            slope = -weight * jnp.where(closing >= 0.0, 1.0, small) / (1.0 + small)
            multiplier.append(weight * (jnp.maximum(closing, 0.0) + jnp.log1p(small)))
        else:
            multiplier.append(slope * change)
        top, rest = halves(three_products(multiplier[f], mortar_rows, NN))
        outbox[4 + f] = dot16(to_bucket, top, NN) + dot16(to_bucket, rest, NN)
        send(4 + f)

    slave_values[...] = jnp.zeros(slave_values.shape, F32)
    for f in range(FIELDS):
        for c in range(3):
            slave_values[:, 3 * f + c, :] = -normal[c] * multiplier[f]
    total = add_rows(slave_values, slave_nodes, slave_right, slaves // 8, node_tiles, total)

    near_copy(ghost_send, ghost_recv, 1, after).wait_recv()
    total = total + dot16(
        left_operand(ghost_recv[...], halo_row, node_tiles), right_operand(halo_row), NT
    )

    master_values[...] = jnp.zeros(master_values.shape, F32)
    at_slot = jnp.transpose(request, (1, 0))[0:1, :]
    to_slot = where01(iota((masters, buckets), 0).astype(F32) == at_slot).astype(BF16)
    for f in range(FIELDS):
        receive(4 + f)
        arrived = inbox[4 + f]
        for c in range(3):
            top, rest = halves(request[:, c + 1 : c + 2] * arrived)
            master_values[:, 3 * f + c, :] = dot16(to_slot, top, NN) + dot16(to_slot, rest, NN)
    total = add_rows(master_values, master_nodes, master_right, masters // 8, node_tiles, total)
    for number in range(node_tiles):
        value = tile_sum(total, number)
        result[0:3, column(number)] = value[0:3] - external_force[:, column(number)]
        result[3:9, column(number)] = value[3:9]

    for phase in range(PHASES):
        sent(phase)
    near_copy(halo_send, halo_recv, 0, before).wait_send()
    near_copy(ghost_send, ghost_recv, 1, after).wait_send()


def on_device(*arguments):
    arguments = list(arguments)
    displacement, slave_nodes, master_nodes = arguments[0], arguments[7], arguments[8]
    arguments[5] = arguments[5].reshape(1, -1)
    arguments[6] = arguments[6].reshape(1, -1)
    arguments[9] = arguments[9].T
    arguments[10] = arguments[10].reshape(1, -1)
    arguments[12] = arguments[12].T
    arguments[14] = arguments[14].T
    node_count = displacement.shape[1]
    slaves, masters = slave_nodes.shape[0], master_nodes.shape[0]
    corners = arguments[4].shape[0]
    layers = lax.axis_size("layer")
    devices = lax.axis_size("mesh") * layers
    capacity = max(2, 2 * slaves // devices)
    share = -(-capacity // 8) * 8
    buckets = devices * share
    vmem = lambda *shape: pltpu.VMEM(shape, F32)
    near = vmem(ROWS, LANES)
    mail = vmem(PHASES, buckets, LANES)
    rights = [pltpu.VMEM((rows // 8, LANES, 8 * LANES), BF16) for rows in (slaves, corners, masters)]
    result = jax.ShapeDtypeStruct((9, node_count), F32)
    result = pl.pallas_call(
        functools.partial(kernel, devices, layers, share),
        out_shape=result,
        in_specs=[pl.BlockSpec(memory_space=pltpu.HBM)] * len(arguments),
        out_specs=pl.BlockSpec(memory_space=pltpu.VMEM),
        scratch_shapes=[pltpu.VMEM(each.shape, each.dtype) for each in arguments]
        + [
            vmem(ROWS, node_count + LANES),
            near,
            near,
            near,
            near,
            mail,
            mail,
            vmem(slaves, ROWS, LANES),
            vmem(corners, ROWS, LANES),
            vmem(masters, ROWS, LANES),
            *rights,
            pltpu.SemaphoreType.DMA((PHASES,)),
            pltpu.SemaphoreType.DMA((PHASES,)),
            pltpu.SemaphoreType.DMA((2,)),
            pltpu.SemaphoreType.DMA((2,)),
            pltpu.SemaphoreType.DMA((len(arguments),)),
        ],
        compiler_params=pltpu.CompilerParams(
            collective_id=0, has_side_effects=True, vmem_limit_bytes=63 * 1024 * 1024
        ),
    )(*arguments)
    return result[0:3], result[3:6], result[6:9]


def solution(mesh):
    split = ("groups", "mesh", "layer")
    wide, flat, tall = P(None, split), P(split), P(split, None)
    return jax.shard_map(
        on_device,
        mesh=mesh,
        in_specs=(wide,) * 5 + (flat, flat) + (tall,) * 3 + (flat,) + (tall,) * 3 + (P(), P()),
        out_specs=(wide, wide, wide),
        check_vma=False,
    )
```

```python
import functools

import jax
import jax.numpy as jnp
from jax import lax
from jax.experimental import pallas as pl
from jax.experimental.pallas import tpu as pltpu
from jax.sharding import PartitionSpec as P

PENALTY = 2.0
HIGH = lax.Precision.HIGHEST
LANES = 128
ROWS = 16
FIELDS = 3
PHASES = 1 + 2 * FIELDS
NN = ((1,), (0,))
NT = ((1,), (1,))
TN = ((0,), (0,))
LOAD_ORDER = (9, 10, 12, 0, 1, 2, 6, 8, 7, 4, 5, 14, 11, 13, 15, 3)
F32 = jnp.float32
BF16 = jnp.bfloat16


def dot(left, right, dims):
    return lax.dot_general(
        left, right, (dims, ((), ())), precision=HIGH, preferred_element_type=F32
    )


def dot16(left, right, dims):
    return lax.dot_general(left, right, (dims, ((), ())), preferred_element_type=F32)


def halves(value):
    top = value.astype(BF16)
    return top, (value - top.astype(F32)).astype(BF16)


def thirds(value):
    top = value.astype(BF16)
    rest = value - top.astype(F32)
    middle = rest.astype(BF16)
    return top, middle, (rest - middle.astype(F32)).astype(BF16)


def iota(shape, dim):
    return lax.broadcasted_iota(jnp.int32, shape, dim)


def where01(mask):
    return jnp.where(mask, 1.0, 0.0).astype(F32)


def column(index, by=LANES):
    return slice(index * by, (index + 1) * by)


def lookup(tile_of, tiles, index):
    lane = jnp.bitwise_and(index, LANES - 1)
    tile = jnp.right_shift(index, 7)
    found = jnp.zeros(index.shape, F32)
    for number in range(tiles):
        table = jnp.broadcast_to(tile_of(number), index.shape)
        picked = jnp.take_along_axis(table, lane, axis=1, mode="promise_in_bounds")
        found = jnp.where(tile == number, picked, found)
    return found


def left_operand(values, index, tiles):
    tile = jnp.right_shift(index, 7)
    top = values.astype(BF16).astype(F32)
    both = jnp.concatenate([top, values - top], axis=0)
    return jnp.concatenate(
        [jnp.where(tile == number, both, 0.0).astype(BF16) for number in range(tiles)], axis=0
    )


def right_operand(index):
    lane = jnp.bitwise_and(index, LANES - 1)
    return where01(lane == iota((LANES, LANES), 0)).astype(BF16)


def eight_rows(index_ref, group):
    return index_ref[pl.ds(pl.multiple_of(group * 8, 8), 8), :]


def fill_right(right_ref, index_ref, groups):
    def step(group, carry):
        rows = eight_rows(index_ref, group)
        for k in range(8):
            right_ref[group, :, column(k)] = right_operand(rows[k : k + 1, :])
        return carry

    lax.fori_loop(0, groups, step, 0)


def add_rows(value_ref, index_ref, right_ref, groups, tiles, total):
    def step(group, total):
        rows = eight_rows(index_ref, group)
        left = [left_operand(value_ref[group * 8 + k], rows[k : k + 1, :], tiles) for k in range(8)]
        return total + dot16(jnp.concatenate(left, axis=1), right_ref[group], NT)

    return lax.fori_loop(0, groups, step, total, unroll=2 if groups > 1 else 1)


def three_products(value, factor, dims):
    top, rest = halves(value)
    return dot16(jnp.concatenate([top, top, rest], axis=1), factor, dims)


def tile_sum(total, number):
    start = number * 2 * ROWS
    return total[start : start + ROWS] + total[start + ROWS : start + 2 * ROWS]


def kernel(
    devices,
    layers,
    share,
    *refs,
):
    sources, outputs, held, scratch = refs[:16], refs[16:17], refs[17:33], refs[33:]
    (
        displacement,
        tangent_one,
        tangent_two,
        external_force,
        connectivity,
        element_scale,
        halo_nodes,
        slave_nodes,
        master_nodes,
        pair_owner,
        pair_slot,
        active_flags,
        normals,
        initial_gap,
        strain_operator,
        mortar,
    ) = held
    (result,) = outputs
    (
        field,
        halo_send,
        halo_recv,
        ghost_send,
        ghost_recv,
        outbox,
        inbox,
        slave_values,
        element_values,
        master_values,
        slave_right,
        element_right,
        master_right,
        send_sem,
        recv_sem,
        near_send_sem,
        near_recv_sem,
        input_sem,
    ) = scratch
    node_count = displacement.shape[1]
    node_tiles = node_count // LANES
    slaves = slave_nodes.shape[0]
    masters = master_nodes.shape[0]
    buckets = devices * share
    group = lax.axis_index("groups")
    me = lax.axis_index("mesh") * layers + lax.axis_index("layer")

    after = lax.rem(me + 1, devices)
    before = lax.rem(me + devices - 1, devices)

    def device(peer):
        return (group, peer // layers, lax.rem(peer, layers))

    def block(ref, phase, peer):
        return ref.at[phase, pl.ds(pl.multiple_of(peer * share, share), share), :]

    def send(phase):
        def one(k, carry):
            peer = lax.rem(me + k, devices)
            pltpu.make_async_remote_copy(
                src_ref=block(outbox, phase, peer),
                dst_ref=block(inbox, phase, me),
                send_sem=send_sem.at[phase],
                recv_sem=recv_sem.at[phase],
                device_id=device(peer),
                device_id_type=pl.DeviceIdType.MESH,
            ).start()
            return carry

        lax.fori_loop(1, devices, one, 0, unroll=devices <= 16)
        mine = pl.ds(pl.multiple_of(me * share, share), share)
        inbox[phase, mine, :] = outbox[phase, mine, :]

    def whole(phase):
        rows = pl.ds(0, buckets - share)
        return pltpu.make_async_remote_copy(
            src_ref=outbox.at[phase, rows, :],
            dst_ref=inbox.at[phase, rows, :],
            send_sem=send_sem.at[phase],
            recv_sem=recv_sem.at[phase],
            device_id=device(after),
            device_id_type=pl.DeviceIdType.MESH,
        )

    def receive(phase):
        whole(phase).wait_recv()

    def sent(phase):
        whole(phase).wait_send()

    def near_copy(source, target, number, peer):
        return pltpu.make_async_remote_copy(
            src_ref=source,
            dst_ref=target,
            send_sem=near_send_sem.at[number],
            recv_sem=near_recv_sem.at[number],
            device_id=device(peer),
            device_id_type=pl.DeviceIdType.MESH,
        )

    barrier = pltpu.get_barrier_semaphore()

    def greet(k, carry):
        pl.semaphore_signal(
            barrier,
            inc=1,
            device_id=device(lax.rem(me + k, devices)),
            device_id_type=pl.DeviceIdType.MESH,
        )
        return carry

    lax.fori_loop(1, devices, greet, 0)

    loads = [
        pltpu.make_async_copy(source, target, input_sem.at[number])
        for number, source, target in zip(range(len(sources)), sources, held)
    ]
    for number in LOAD_ORDER:
        loads[number].start()

    def ready(*numbers):
        for number in numbers:
            loads[number].wait()

    ready(9, 10, 12)
    first = iota((slaves, slaves), 0)
    second = iota((slaves, slaves), 1)

    def stand(row):
        return jnp.sum(jnp.where(first == second, row, 0.0), axis=1, keepdims=True)

    owner_row = pair_owner[...].astype(F32)
    owner_column = stand(owner_row)
    slot_column = stand(pair_slot[...].astype(F32))
    normal = [stand(normals[c : c + 1, :]) for c in range(3)]
    same = where01(owner_column == owner_row)
    rank_row = jnp.sum(jnp.where(first < second, same, 0.0), axis=0, keepdims=True)
    rank_column = jnp.sum(jnp.where(second < first, same, 0.0), axis=1, keepdims=True)
    bucket_row = owner_row * share + rank_row
    bucket_column = owner_column * share + rank_column
    to_bucket = where01(iota((buckets, slaves), 0).astype(F32) == bucket_row)
    lane = iota((slaves, LANES), 1)
    wanted = jnp.where(lane == 0, slot_column, 0.0)
    for c in range(3):
        wanted = jnp.where(lane == c + 1, normal[c], wanted)
    outbox[0] = dot(to_bucket, wanted, NN)

    field[...] = jnp.zeros(field.shape, F32)
    ready(0, 1, 2, 6)
    for f, source in enumerate((displacement, tangent_one, tangent_two)):
        field[3 * f : 3 * f + 3, 0:node_count] = source[...]
    ghosts = halo_nodes.shape[1]
    halo_row = jnp.concatenate(
        [halo_nodes[...], jnp.full((1, LANES - ghosts), node_count, jnp.int32)], axis=1
    )
    halo_send[...] = lookup(
        lambda number: field[:, column(number)],
        node_tiles,
        jnp.broadcast_to(halo_row, (ROWS, LANES)),
    )


    def nodal(index, fc):
        return lookup(lambda number: field[fc : fc + 1, column(number)], node_tiles, index)

    ready(8)
    master_index = master_nodes[...]
    parts = [thirds(nodal(master_index, fc)) for fc in range(9)]
    served = jnp.concatenate(
        [jnp.concatenate([part[k] for part in parts], axis=1) for k in range(3)], axis=0
    )
    ready(7)
    slave_index = slave_nodes[...]
    slave_normal = []
    for f in range(FIELDS):
        value = normal[0] * nodal(slave_index, 3 * f)
        for c in range(1, 3):
            value = value + normal[c] * nodal(slave_index, 3 * f + c)
        slave_normal.append(value)

    pl.semaphore_wait(barrier, devices - 1)
    send(0)
    near_copy(halo_send, halo_recv, 0, before).start()

    ready(4, 5, 11, 13, 14, 15, 3)
    live = jnp.where(slave_index < node_count, PENALTY, 0.0)
    weight = active_flags[...].astype(F32) * live
    top, rest = halves(mortar[...])
    mortar_rows = jnp.concatenate([top, rest, top], axis=0)
    mortar_columns = jnp.concatenate([top, rest, top], axis=1)
    fill_right(slave_right, slave_nodes, slaves // 8)
    fill_right(element_right, connectivity, 1)
    fill_right(master_right, master_nodes, masters // 8)

    receive(0)
    request = inbox[0]
    pick = where01(
        lax.rem(iota((buckets, 3 * masters), 1), masters).astype(F32) == request[:, 0:1]
    ).astype(BF16)
    for f in range(FIELDS):
        chosen = dot16(pick, served[:, column(f, 3 * LANES)], NN)
        value = request[:, 1:2] * chosen[:, column(0)]
        for c in range(1, 3):
            value = value + request[:, c + 1 : c + 2] * chosen[:, column(c)]
        outbox[1 + f] = value
        send(1 + f)

    near_copy(halo_send, halo_recv, 0, before).wait_recv()
    field[:, node_count : node_count + LANES] = halo_recv[...]
    corner = connectivity[...]
    elements = jnp.concatenate(
        [
            jnp.concatenate(
                [
                    lookup(
                        lambda number: field[3 * f + c : 3 * f + c + 1, column(number)],
                        node_tiles + 1,
                        corner,
                    )
                    for c in range(3)
                ],
                axis=0,
            )
            for f in range(FIELDS)
        ],
        axis=1,
    )
    entries = strain_operator.shape[0]
    order = iota((entries, entries), 0)
    operator = dot(
        where01(iota((entries, entries), 1) == 3 * lax.rem(order, 8) + order // 8),
        strain_operator[...],
        NN,
    )
    strain = dot(operator, elements, TN)
    scale = element_scale[...]
    base = strain[:, 0:LANES]
    hyperbolic = jnp.tanh(base)
    stiffness = scale * (1.0 + 0.5 * (1.0 - hyperbolic * hyperbolic))
    stress = jnp.concatenate(
        [
            scale * (base + 0.5 * hyperbolic),
            stiffness * strain[:, column(1)],
            stiffness * strain[:, column(2)],
        ],
        axis=1,
    )
    element_force = dot(operator, stress, NN)
    element_values[...] = jnp.zeros(element_values.shape, F32)
    for f in range(FIELDS):
        for c in range(3):
            element_values[:, 3 * f + c, :] = element_force[8 * c : 8 * c + 8, column(f)]
    total = jnp.zeros((2 * ROWS * (node_tiles + 1), LANES), F32)
    total = add_rows(element_values, connectivity, element_right, 1, node_tiles + 1, total)
    ghost_send[...] = tile_sum(total, node_tiles)
    near_copy(ghost_send, ghost_recv, 1, after).start()
    total = total[: 2 * ROWS * node_tiles]

    from_bucket = where01(iota((slaves, buckets), 1).astype(F32) == bucket_column).astype(BF16)
    to_bucket = to_bucket.astype(BF16)
    multiplier = []
    slope = None
    for f in range(FIELDS):
        receive(1 + f)
        top, rest = halves(inbox[1 + f])
        fetched = dot16(from_bucket, top, NN) + dot16(from_bucket, rest, NN)
        change = slave_normal[f] - three_products(fetched, mortar_columns, NT)
        if f == 0:
            closing = -(initial_gap[...] + change)
            small = jnp.exp(-jnp.abs(closing))
            slope = -weight * jnp.where(closing >= 0.0, 1.0, small) / (1.0 + small)
            multiplier.append(weight * (jnp.maximum(closing, 0.0) + jnp.log1p(small)))
        else:
            multiplier.append(slope * change)
        top, rest = halves(three_products(multiplier[f], mortar_rows, NN))
        outbox[4 + f] = dot16(to_bucket, top, NN) + dot16(to_bucket, rest, NN)
        send(4 + f)

    slave_values[...] = jnp.zeros(slave_values.shape, F32)
    for f in range(FIELDS):
        for c in range(3):
            slave_values[:, 3 * f + c, :] = -normal[c] * multiplier[f]
    total = add_rows(slave_values, slave_nodes, slave_right, slaves // 8, node_tiles, total)

    near_copy(ghost_send, ghost_recv, 1, after).wait_recv()
    total = total + dot16(
        left_operand(ghost_recv[...], halo_row, node_tiles), right_operand(halo_row), NT
    )

    master_values[...] = jnp.zeros(master_values.shape, F32)
    at_slot = jnp.transpose(request, (1, 0))[0:1, :]
    to_slot = where01(iota((masters, buckets), 0).astype(F32) == at_slot).astype(BF16)
    for f in range(FIELDS):
        receive(4 + f)
        arrived = inbox[4 + f]
        for c in range(3):
            top, rest = halves(request[:, c + 1 : c + 2] * arrived)
            master_values[:, 3 * f + c, :] = dot16(to_slot, top, NN) + dot16(to_slot, rest, NN)
    total = add_rows(master_values, master_nodes, master_right, masters // 8, node_tiles, total)
    for number in range(node_tiles):
        value = tile_sum(total, number)
        result[0:3, column(number)] = value[0:3] - external_force[:, column(number)]
        result[3:9, column(number)] = value[3:9]

    for phase in range(PHASES):
        sent(phase)
    near_copy(halo_send, halo_recv, 0, before).wait_send()
    near_copy(ghost_send, ghost_recv, 1, after).wait_send()


def on_device(*arguments):
    arguments = list(arguments)
    displacement, slave_nodes, master_nodes = arguments[0], arguments[7], arguments[8]
    arguments[5] = arguments[5].reshape(1, -1)
    arguments[6] = arguments[6].reshape(1, -1)
    arguments[9] = arguments[9].T
    arguments[10] = arguments[10].reshape(1, -1)
    arguments[12] = arguments[12].T
    arguments[14] = arguments[14].T
    node_count = displacement.shape[1]
    slaves, masters = slave_nodes.shape[0], master_nodes.shape[0]
    corners = arguments[4].shape[0]
    layers = lax.axis_size("layer")
    devices = lax.axis_size("mesh") * layers
    capacity = max(2, 2 * slaves // devices)
    share = -(-capacity // 8) * 8
    buckets = devices * share
    vmem = lambda *shape: pltpu.VMEM(shape, F32)
    near = vmem(ROWS, LANES)
    mail = vmem(PHASES, buckets, LANES)
    rights = [pltpu.VMEM((rows // 8, LANES, 8 * LANES), BF16) for rows in (slaves, corners, masters)]
    result = jax.ShapeDtypeStruct((9, node_count), F32)
    result = pl.pallas_call(
        functools.partial(kernel, devices, layers, share),
        out_shape=result,
        in_specs=[pl.BlockSpec(memory_space=pltpu.HBM)] * len(arguments),
        out_specs=pl.BlockSpec(memory_space=pltpu.VMEM),
        scratch_shapes=[pltpu.VMEM(each.shape, each.dtype) for each in arguments]
        + [
            vmem(ROWS, node_count + LANES),
            near,
            near,
            near,
            near,
            mail,
            mail,
            vmem(slaves, ROWS, LANES),
            vmem(corners, ROWS, LANES),
            vmem(masters, ROWS, LANES),
            *rights,
            pltpu.SemaphoreType.DMA((PHASES,)),
            pltpu.SemaphoreType.DMA((PHASES,)),
            pltpu.SemaphoreType.DMA((2,)),
            pltpu.SemaphoreType.DMA((2,)),
            pltpu.SemaphoreType.DMA((len(arguments),)),
        ],
        compiler_params=pltpu.CompilerParams(
            collective_id=0, has_side_effects=True, vmem_limit_bytes=63 * 1024 * 1024
        ),
    )(*arguments)
    return result[0:3], result[3:6], result[6:9]


def solution(mesh):
    split = ("groups", "mesh", "layer")
    wide, flat, tall = P(None, split), P(split), P(split, None)
    return jax.shard_map(
        on_device,
        mesh=mesh,
        in_specs=(wide,) * 5 + (flat, flat) + (tall,) * 3 + (flat,) + (tall,) * 3 + (P(), P()),
        out_specs=(wide, wide, wide),
        check_vma=False,
    )
```
